128 devices in a mesh: dp: 16 (over y, z), expert: 8 (over x, core).
Axes of the slice: x: 4, y: 4, z: 4, core: 2. Of those that a mesh axis runs over, the one named last changes fastest.
Arguments:
- block_input: bfloat16 [16384, 1024], P(('dp', 'expert')), may hold values from -6 to 6
- attn_gain: float32 [1024], replicated, may hold values from 0.1 to 1.9
- query_weight: bfloat16 [1024, 1024], P('dp', 'expert'), may hold values from -0.1875 to 0.1875
- kv_weight: bfloat16 [1024, 1024], P('dp', 'expert'), may hold values from -0.1875 to 0.1875
- out_weight: bfloat16 [1024, 1024], P('dp', 'expert'), may hold values from -1.5 to 1.5
- moe_gain: float32 [1024], replicated, may hold values from 0.1 to 1.9
- router_weight: float32 [1024, 32], replicated, may hold values from -0.09375 to 0.09375
- expert_gate: bfloat16 [32, 1024, 512], P('expert', 'dp'), may hold values from -0.1875 to 0.1875
- expert_up: bfloat16 [32, 1024, 512], P('expert', 'dp'), may hold values from -0.1875 to 0.1875
- expert_down: bfloat16 [32, 1024, 512], P('expert', 'dp'), may hold values from -0.75 to 0.75
- routes: int32 [16384, 8], P(('dp', 'expert')), may hold values from 0 to 31, all different within a row; in each aligned block of 128 rows (0 to 127, 128 to 255, ...) at most 48 rows name the same one
- seq_lengths: int32 [16, 4], P('dp'), may hold values from 1 to 960, 1024 in all within a row
- out_grad: bfloat16 [16384, 1024], P(('dp', 'expert')), may hold values from -6 to 6
Outputs:
- block_out: bfloat16 [16384, 1024], P(('dp', 'expert'))
- input_grad: float32 [16384, 1024], P(('dp', 'expert'))
- attn_gain_grad: float32 [1024], replicated
- query_grad: float32 [1024, 1024], P('dp', 'expert')
- kv_grad: float32 [1024, 1024], P('dp', 'expert')
- out_weight_grad: float32 [1024, 1024], P('dp', 'expert')
- moe_gain_grad: float32 [1024], replicated
- router_grad: float32 [1024, 32], replicated
- gate_grad: float32 [32, 1024, 512], P('expert', 'dp')
- up_grad: float32 [32, 1024, 512], P('expert', 'dp')
- down_grad: float32 [32, 1024, 512], P('expert', 'dp')
The draws below stay inside these ranges and needn't reach their ends.
Inputs may be any that keep to these rules, and one draw needn't show every extreme that they name: `routes`: each token names 8 different experts. Among the tokens of one device (aligned blocks of 128 rows), no expert is named by more than 48 of them, and in every draw some expert is named by exactly 48 in some block. `seq_lengths`: each row sums to 1024; the longest sequence of every group has exactly 960 tokens.
All inputs are finite; a program needn't handle non-finite values.
Results may differ from the reference program's by a relative error of at most 0.028.
Values may be sent and summed in bfloat16 or wider, within the bound.
A program may use at most 128 MiB of HBM per device.

```python
import math
import jax
import jax.numpy as jnp
import numpy as np
from jax import lax

D = 1024
HEADS = 16
KV_HEADS = 8
HEAD_DIM = 64
FF = 512
TOP = 8
GROUP_TOK = 1024
SEQS = 4
QW = 1024
KW = 512
EXPERTS = 32
GROUPS = 16
TOK_DEV = 128
TOKENS = 16384
BLOCKS = 128
CAP = 48


def steps_of(key, shape, pieces, least, top_value):
    def one(axis_at, shards_of):
        draws = jax.random.uniform(jax.random.fold_in(jax.random.fold_in(key, 6), axis_at), (shards_of,), jnp.float32, least / len(pieces), top_value / len(pieces))
        return jnp.repeat(jnp.exp(draws), shape[axis_at] // shards_of).reshape((-1,) + (1,) * (len(shape) - axis_at - 1))

    gain = one(*pieces[0])
    for cut in pieces[1:]:
        gain = gain * one(*cut)
    return gain


def split_up(amount, total, most, lean):
    weights = [(1 << 20) // math.isqrt(standing ** lean) + 1 for standing in range(2, amount + 1)]
    rest, counts = total - most - (amount - 1), [1] * (amount - 1)
    while rest > 0:
        candidates = [i for i in range(amount - 1) if counts[i] < most]
        whole, budget = sum([weights[i] for i in candidates]), rest
        for i in candidates:
            extra = min(most - counts[i], max(1, budget * weights[i] // whole), rest)
            counts[i] = counts[i] + extra
            rest = rest - extra
    return np.array([most] + counts)


def uneven_parts(own_key, count, total, reach, skew):
    if count == 2:
        one = jax.random.randint(own_key, (), max(1, total - reach), min(reach, total - 1) + 1)
        return jnp.stack([one, total - one])
    tallies = jnp.asarray(split_up(count, total, reach, skew), jnp.int32)
    pairs = (count - 1) // 2
    giver, receiver = tallies[1:1 + 2 * pairs:2], tallies[2:2 + 2 * pairs:2]
    slack = jnp.minimum(giver - 1, reach - receiver)
    passed = jax.random.randint(jax.random.fold_in(own_key, 1), (pairs,), 0, 1 << 20) % (slack + 1)
    tallies = tallies.at[1:1 + 2 * pairs:2].set(giver - passed).at[2:2 + 2 * pairs:2].set(receiver + passed)
    return tallies[jax.random.permutation(jax.random.fold_in(own_key, 2), count)]


def shared_out(rng, own, number, rows, number_of, top, most, slope):
    ranking = jax.random.permutation(rng, number_of)
    crowded, common = portions_of(number_of, rows * top, most, slope, True), portions_of(number_of, rows * top, most, slope, False)
    places = jnp.arange(number_of)

    def named(sizes, offset_by):
        used = int((sizes > 0).sum())
        fixed = max(1, used // 4)
        shifted = fixed + (places - fixed + offset_by * (used - fixed)) % max(1, number_of - fixed)
        return jnp.zeros((number_of,), jnp.int32).at[ranking[jnp.where(places < fixed, places, shifted)]].set(jnp.asarray(sizes, jnp.int32))

    sizes = jnp.where(number % 4 == 0, named(crowded, number // 4), named(common, number - number // 4 - 1))
    mixed = jax.random.permutation(jax.random.fold_in(own, 3), number_of)
    giver, receiver = mixed[0:number_of // 2 * 2:2], mixed[1:number_of // 2 * 2:2]
    room = jnp.minimum(sizes[giver] - 1, most - sizes[receiver]) // 2
    room = jnp.where((giver == ranking[0]) | (receiver == ranking[0]) | (sizes[receiver] == 0), 0, jnp.maximum(room, 0))
    shifted = jax.random.randint(jax.random.fold_in(own, 4), (number_of // 2,), 0, 1 << 20) % (room + 1)
    sizes = sizes.at[giver].add(-shifted).at[receiver].add(shifted)
    items = jnp.searchsorted(jnp.cumsum(sizes), jnp.arange(rows * top), side="right").astype(jnp.int32)
    table = items.reshape(top, rows).T
    table = table[jax.random.permutation(jax.random.fold_in(own, 1), rows)]
    offset_by = jax.random.randint(jax.random.fold_in(own, 2), (rows, 1), 0, top)
    return jnp.take_along_axis(table, (jnp.arange(top)[None, :] + offset_by) % top, axis=1)


def portions_of(number_of, total, most, slope, full):
    portions = [(1 << 20) // math.isqrt(grade ** slope) + 1 for grade in range(1, number_of + 1)]
    largest = most if full else min(most, max(-(-total // number_of), total * portions[0] // sum(portions)))
    least = 1 if total - largest >= number_of - 1 else 0
    holding, spare = [largest] + [least] * (number_of - 1), total - largest - least * (number_of - 1)
    while spare > 0:
        candidates = [i for i in range(1, number_of) if holding[i] < largest] or [i for i in range(1, number_of) if holding[i] < most]
        whole, budget = sum([portions[i] for i in candidates]), spare
        for i in candidates:
            more = min(most - holding[i], max(1, budget * portions[i] // whole), spare)
            holding[i] = holding[i] + more
            spare = spare - more
    return np.array(holding)


def normal_values(key, shape, spread, bound, shards=(), kind=jnp.bfloat16):
    entries = jax.random.normal(key, shape, jnp.float32) * spread
    if len(shards) > 0:
        entries = steps_of(key, shape, shards, -0.22, 0.18) * entries
    return jnp.clip(entries, min=-bound, max=bound).astype(kind)


def setup_inputs(seed: int = 0) -> dict:
    key_list = jax.random.split(jax.random.key(seed), 14)
    block_input = normal_values(key_list[0], (TOKENS, D), 1.0, 6.0, ((0, 128),))
    attn_gain = jnp.clip(1.0 + 0.18 * jax.random.normal(key_list[1], (D,), jnp.float32), 0.1, 1.9)
    query_weight = normal_values(key_list[2], (D, QW), D ** -0.5, 0.1875, ((0, 16), (1, 8)))
    kv_weight = normal_values(key_list[3], (D, 2 * KW), D ** -0.5, 0.1875, ((0, 16), (1, 8)))
    out_weight = normal_values(key_list[4], (D, QW), (QW // 64) ** -0.5, 1.5, ((0, 16), (1, 8)))
    moe_gain = jnp.clip(1.0 + 0.18 * jax.random.normal(key_list[5], (D,), jnp.float32), 0.1, 1.9)
    router_weight = normal_values(key_list[6], (D, EXPERTS), (4 * D) ** -0.5, 0.09375, (), jnp.float32)
    expert_gate = normal_values(key_list[7], (EXPERTS, D, FF), D ** -0.5, 0.1875, ((0, 8), (1, 16)))
    expert_up = normal_values(key_list[8], (EXPERTS, D, FF), D ** -0.5, 0.1875, ((0, 8), (1, 16)))
    expert_down = normal_values(key_list[9], (EXPERTS, D, FF), (FF // 8) ** -0.5, 0.75, ((0, 8), (1, 16)))
    routes_keys = jax.random.split(jax.random.fold_in(key_list[10], 1), TOKENS // TOK_DEV)
    routes_turns = jax.random.permutation(jax.random.fold_in(key_list[10], 3), TOKENS // TOK_DEV)
    routes = jax.vmap(lambda own, number: shared_out(jax.random.fold_in(key_list[10], 2), own, number, TOK_DEV, EXPERTS, TOP, CAP, 1))(routes_keys, routes_turns).reshape((TOKENS, TOP))
    seq_lengths = jax.vmap(lambda own: uneven_parts(own, SEQS, GROUP_TOK, GROUP_TOK - TOK_DEV // 2, 0))(jax.random.split(key_list[11], GROUPS)).reshape((GROUPS, SEQS)).astype(jnp.int32)
    out_grad = normal_values(key_list[12], (TOKENS, D), 1.0, 6.0, ((0, 128),))
    return dict(block_input=block_input, attn_gain=attn_gain, query_weight=query_weight, kv_weight=kv_weight, out_weight=out_weight, moe_gain=moe_gain, router_weight=router_weight, expert_gate=expert_gate, expert_up=expert_up, expert_down=expert_down, routes=routes, seq_lengths=seq_lengths, out_grad=out_grad)


@jax.custom_vjp
def low(v):
    return lax.optimization_barrier(v.astype(jnp.bfloat16)).astype(jnp.float32)

@jax.custom_vjp
def low_back(v):
    return v

def low_keep(v):
    return (low(v), None)

def low_pass(kept, grad):
    return (grad,)

def back_keep(v):
    return (v, None)

def back_low(kept, grad):
    return (low(grad),)
low.defvjp(low_keep, low_pass)
low_back.defvjp(back_keep, back_low)
HIGH = lax.Precision.HIGHEST
eps_norm = 1e-06
rope_base = 10000.0

def rms_scale(v):
    return lax.rsqrt(lax.optimization_barrier(jnp.mean(v * v, axis=-1, keepdims=True)) + eps_norm)

def rotate(v, cosine, sine):
    half = v.shape[-1] // 2
    first = v[..., :half]
    second = v[..., half:]
    return jnp.concatenate([first * cosine - second * sine, second * cosine + first * sine], axis=-1)

def group_layout(lengths):
    ends = jnp.cumsum(lengths).astype(jnp.int32)
    starts = ends - lengths
    places = jnp.arange(GROUP_TOK, dtype=jnp.int32)
    segment = lax.optimization_barrier(jnp.sum((places[:, None] >= ends[None, :]).astype(jnp.int32), axis=1))
    labels = jnp.arange(SEQS, dtype=jnp.int32)
    begin = lax.optimization_barrier(jnp.sum(jnp.where(segment[:, None] == labels[None, :], starts[None, :], 0), axis=1))
    return (segment, places - begin)

def slot_table(block_routes):
    flat = block_routes.reshape(-1)
    chosen = (flat[:, None] == jnp.arange(EXPERTS, dtype=jnp.int32)[None, :]).astype(jnp.int32)
    before = jnp.cumsum(chosen, axis=0) - chosen
    rank = lax.optimization_barrier(jnp.sum(before * chosen, axis=1))
    position = flat * CAP + rank
    owner = jnp.full((EXPERTS * CAP,), TOK_DEV, jnp.int32)
    owner = owner.at[position].set(jnp.arange(TOK_DEV * TOP, dtype=jnp.int32) // TOP)
    return (position, owner)

def attend_group(args):
    query, key, value, lengths = args
    segment, place = group_layout(lengths)
    every = jnp.arange(GROUP_TOK, dtype=jnp.int32)
    allowed = (segment[:, None] == segment[None, :]) & (every[None, :] <= every[:, None])
    grouped = HEADS // KV_HEADS
    heads = query.reshape(GROUP_TOK, KV_HEADS, grouped, HEAD_DIM)
    scores = jnp.einsum('qkgd,skd->kgqs', heads, key, precision=HIGH) * HEAD_DIM ** (-0.5)
    scores = low_back(scores)
    scores = jnp.where(allowed, scores, -1e+30)
    top = lax.optimization_barrier(jnp.max(scores, axis=-1, keepdims=True))
    expo = jnp.exp(scores - top)
    probs = low(expo / lax.optimization_barrier(jnp.sum(expo, axis=-1, keepdims=True)))
    mixed = jnp.einsum('kgqs,skd->qkgd', probs, value, precision=HIGH)
    return mixed.reshape(GROUP_TOK, QW)

def reference(block_input, attn_gain, query_weight, kv_weight, out_weight, moe_gain, router_weight, expert_gate, expert_up, expert_down, routes, seq_lengths, out_grad):
    half = HEAD_DIM // 2
    inv_freq = jnp.exp(-jnp.log(rope_base) * 2.0 * jnp.arange(half, dtype=jnp.float32) / HEAD_DIM)
    places = jax.vmap(lambda lengths: group_layout(lengths)[1])(seq_lengths).reshape(TOKENS)
    angle = places.astype(jnp.float32)[:, None] * inv_freq[None, :]
    cosine = jnp.cos(angle)[:, None, :]
    sine = jnp.sin(angle)[:, None, :]
    position, owner = jax.vmap(slot_table)(routes.reshape(BLOCKS, TOK_DEV, TOP))

    def forward(x, gain1, w_query, w_kv, w_out, gain2, w_router, w_gate, w_up, w_down):
        normed1 = low(x * rms_scale(x) * gain1)
        q_lin = low_back(jnp.dot(normed1, w_query, precision=HIGH))
        kv_lin = low_back(jnp.dot(normed1, w_kv, precision=HIGH)).reshape(TOKENS, KV_HEADS, 2, HEAD_DIM)
        query = low(rotate(q_lin.reshape(TOKENS, HEADS, HEAD_DIM), cosine, sine))
        key = low(rotate(kv_lin[:, :, 0], cosine, sine))
        value = low(kv_lin[:, :, 1])
        mixed = lax.map(jax.checkpoint(attend_group), (query.reshape(GROUPS, GROUP_TOK, HEADS, HEAD_DIM), key.reshape(GROUPS, GROUP_TOK, KV_HEADS, HEAD_DIM), value.reshape(GROUPS, GROUP_TOK, KV_HEADS, HEAD_DIM), seq_lengths))
        mixed = low_back(low(mixed.reshape(TOKENS, QW)))
        attn = low_back(jnp.dot(mixed, w_out.T, precision=HIGH))
        h_one = x + attn
        normed2 = low(h_one * rms_scale(h_one) * gain2)
        logits = jnp.dot(normed2, w_router, precision=HIGH)
        picked = jnp.take_along_axis(logits, routes, axis=1)
        top = lax.optimization_barrier(jnp.max(picked, axis=1, keepdims=True))
        expo = jnp.exp(picked - top)
        gates = expo / lax.optimization_barrier(jnp.sum(expo, axis=1, keepdims=True))

        def expert_block(args):
            rows, block_gates, block_position, block_owner = args
            padded = jnp.concatenate([rows, jnp.zeros((1, D), jnp.float32)], axis=0)
            taken = low_back(padded[block_owner].reshape(EXPERTS, CAP, D))
            gate_in = low_back(jnp.einsum('ecd,edf->ecf', taken, w_gate, precision=HIGH))
            up_in = low_back(jnp.einsum('ecd,edf->ecf', taken, w_up, precision=HIGH))
            hidden = low(gate_in * jax.nn.sigmoid(gate_in) * up_in)
            result = low_back(low(jnp.einsum('ecf,edf->ecd', hidden, w_down, precision=HIGH)))
            routed = result.reshape(EXPERTS * CAP, D)[block_position].reshape(TOK_DEV, TOP, D)
            return lax.optimization_barrier(jnp.sum(block_gates[:, :, None] * routed, axis=1))
        moe = lax.map(jax.checkpoint(expert_block), (normed2.reshape(BLOCKS, TOK_DEV, D), gates.reshape(BLOCKS, TOK_DEV, TOP), position, owner))
        return h_one + moe.reshape(TOKENS, D)
    primals = (block_input.astype(jnp.float32), attn_gain, query_weight.astype(jnp.float32), kv_weight.astype(jnp.float32), out_weight.astype(jnp.float32), moe_gain, router_weight, expert_gate.astype(jnp.float32), expert_up.astype(jnp.float32), expert_down.astype(jnp.float32))
    result, pullback = jax.vjp(forward, *primals)
    grads = pullback(out_grad.astype(jnp.float32))
    return (result.astype(jnp.bfloat16), grads[0], grads[1], grads[2], grads[3], grads[4], grads[5], grads[6], grads[7], grads[8], grads[9])
```

```python
import functools

import jax
import jax.numpy as jnp
from jax import lax
from jax.experimental import pallas as pl
from jax.experimental.pallas import tpu as pltpu
from jax.sharding import PartitionSpec as P

HEAD_DIM = 64
HIGH = lax.Precision.HIGHEST
eps_norm = 1e-06
rope_base = 10000.0
f32 = jnp.float32
bf16 = jnp.bfloat16
NT = (((1,), (1,)), ((), ()))
TN = (((0,), (0,)), ((), ()))
QB = 256
CAP = 48
VMEM_LIMIT = 60 * 1024 * 1024


def rms_scale(v):
    return lax.rsqrt(jnp.mean(v * v, axis=-1, keepdims=True) + eps_norm)


def mm(a, b, dims=(((1,), (0,)), ((), ()))):
    return lax.dot_general(a, b, dims, preferred_element_type=f32)


def vmem():
    return pl.BlockSpec(memory_space=pltpu.VMEM)


def lanes(shape):
    return lax.broadcasted_iota(jnp.int32, shape, len(shape) - 1)


def swap_halves(v):
    low = (lanes(v.shape) & 32) == 0
    return jnp.where(low, pltpu.roll(v, 96, 1), pltpu.roll(v, 32, 1))


MESH = pl.DeviceIdType.MESH
TOK = 128
HALF = TOK // 2
RING = 4
DEVS = 8
GROUPS = 16


class Place:
    def __init__(self):
        self.me, self.dp = lax.axis_index("expert"), lax.axis_index("dp")
        self.chip, self.core = lax.div(self.me, 2), lax.rem(self.me, 2)
        self.y, self.z = lax.div(self.dp, RING), lax.rem(self.dp, RING)

    def at(self, step, other=False):
        return lax.rem(self.chip + step, RING) * 2 + (1 - self.core if other else self.core)

    def x_to(self, step, other=False):
        return {"expert": self.at(step, other)}

    def y_to(self, step):
        return {"dp": lax.rem(self.y + step, RING) * RING + self.z}

    def z_to(self, step):
        return {"dp": self.y * RING + lax.rem(self.z + step, RING)}


def greet(peers):
    barrier = pltpu.get_barrier_semaphore()
    for peer in peers:
        pl.semaphore_signal(barrier, inc=1, device_id=peer, device_id_type=MESH)
    pl.semaphore_wait(barrier, len(peers))


class Net:
    def __init__(self, send, recv):
        self.send, self.recv, self.used, self.sent = send, recv, 0, []

    def take(self, count):
        self.used += count
        return self.used - count

    def copy(self, src, dst, to, slot):
        return pltpu.make_async_remote_copy(
            src_ref=src, dst_ref=dst, send_sem=self.send.at[slot], recv_sem=self.recv.at[slot],
            device_id=to, device_id_type=MESH)

    def start(self, src, dst, to, slot=None):
        copy = self.copy(src, dst, to, self.take(1) if slot is None else slot)
        copy.start()
        self.sent.append(copy)
        return copy

    def drain(self):
        for copy in self.sent:
            copy.wait_send()

    def drain_some(self, copies):
        for copy in copies:
            copy.wait_send()
            self.sent = [other for other in self.sent if other is not copy]


def shard(buf, index, half=None):
    first = index * TOK + (HALF if half == 1 else 0)
    count = TOK if half is None else HALF
    return buf.at[pl.ds(pl.multiple_of(first, HALF), count), :]


class Gather:
    def __init__(self, net, place, buf):
        self.net, self.place, self.buf, self.sent = net, place, buf, []

    def send(self, index, to, half=None):
        piece = shard(self.buf, index, half)
        self.sent.append(self.net.start(piece, piece, to))
        return self.sent[-1]

    def drain(self):
        self.net.drain_some(self.sent)

    def start(self):
        p = self.place
        self.from_left = self.send(p.me, p.x_to(1))
        self.from_right = self.send(p.me, p.x_to(3))
        self.from_sib = self.send(p.me, p.x_to(0, True))

    def relay(self):
        p, sib = self.place, self.place.x_to(0, True)
        self.from_left.wait_recv()
        self.top = self.send(p.at(3), p.x_to(1), 0)
        self.left_sib = self.send(p.at(3), sib)
        self.from_right.wait_recv()
        self.bottom = self.send(p.at(1), p.x_to(3), 1)
        self.right_sib = self.send(p.at(1), sib)

    def last(self):
        p, sib = self.place, self.place.x_to(0, True)
        self.top.wait_recv()
        self.top_sib = self.send(p.at(2), sib, 0)
        self.bottom.wait_recv()
        self.bottom_sib = self.send(p.at(2), sib, 1)

    def finish(self):
        for copy in (self.from_sib, self.left_sib, self.right_sib, self.top_sib, self.bottom_sib):
            copy.wait_recv()


def scatter_scratch():
    return [pltpu.VMEM((RING, TOK, 1024), bf16), pltpu.VMEM((RING, TOK, 1024), bf16),
            pltpu.VMEM((2, HALF, 1024), bf16), pltpu.VMEM((2, TOK, 1024), bf16)]


class Scatter:
    def __init__(self, net, place, part, scratch):
        self.net, self.place, self.part = net, place, part
        self.from_sib, self.mine, self.halves, self.fulls = scratch
        self.slots = net.take(RING)

    def start(self, chip):
        src = shard(self.part, 2 * chip + 1 - self.place.core)
        self.net.start(src, self.from_sib.at[chip], self.place.x_to(0, True), self.slots + chip)

    def chip_sum(self, step):
        p = self.place
        index = p.at(step)
        chip = lax.div(index, 2)
        src = shard(self.part, index)
        self.net.copy(src, self.from_sib.at[chip], p.x_to(0, True), self.slots + chip).wait_recv()
        self.mine[step] = (src[...].astype(f32) + self.from_sib[chip].astype(f32)).astype(bf16)

    def send(self, step, half, dst, to):
        return self.net.start(self.mine.at[step, pl.ds(half * HALF, HALF), :], dst, to)

    def far(self):
        p = self.place
        self.chip_sum(2)
        self.via_right = self.send(2, 0, self.halves.at[0], p.x_to(1))
        self.via_left = self.send(2, 1, self.halves.at[1], p.x_to(3))
        self.chip_sum(1)
        self.right_bottom = self.send(1, 1, self.fulls.at[0, pl.ds(HALF, HALF), :], p.x_to(1))
        self.chip_sum(3)
        self.left_top = self.send(3, 0, self.fulls.at[1, pl.ds(0, HALF), :], p.x_to(3))
        self.chip_sum(0)

    def near(self):
        p = self.place
        self.via_right.wait_recv()
        self.mine[1, :HALF] = (self.mine[1, :HALF].astype(f32) + self.halves[0].astype(f32)).astype(bf16)
        self.right_top = self.send(1, 0, self.fulls.at[0, pl.ds(0, HALF), :], p.x_to(1))
        self.via_left.wait_recv()
        self.mine[3, HALF:] = (self.mine[3, HALF:].astype(f32) + self.halves[1].astype(f32)).astype(bf16)
        self.left_bottom = self.send(3, 1, self.fulls.at[1, pl.ds(HALF, HALF), :], p.x_to(3))

    def finish(self):
        for copy in (self.right_bottom, self.left_top, self.right_top, self.left_bottom):
            copy.wait_recv()
        return self.mine[0].astype(f32) + self.fulls[0].astype(f32) + self.fulls[1].astype(f32)


class RingGather:
    def __init__(self, net, piece, pos, to):
        self.net, self.piece, self.pos, self.to, self.sent = net, piece, pos, to, []

    def send(self, step, half, to):
        piece = self.piece(lax.rem(self.pos + step, RING), half)
        self.sent.append(self.net.start(piece, piece, self.to(to)))
        return self.sent[-1]

    def drain(self):
        self.net.drain_some(self.sent)

    def start(self):
        self.from_left, self.from_right = self.send(0, None, 1), self.send(0, None, 3)
        return self

    def relay(self):
        self.from_left.wait_recv()
        self.top = self.send(3, 0, 1)
        self.from_right.wait_recv()
        self.bottom = self.send(1, 1, 3)

    def finish(self):
        self.top.wait_recv()
        self.bottom.wait_recv()


def ring_scratch(shape):
    half = (shape[0] // 2, *shape[1:])
    return [pltpu.VMEM((2, *half), bf16), pltpu.VMEM((2, *half), bf16), pltpu.VMEM((2, 2, *half), bf16)]


def chunks(count):
    if count <= RING:
        return count, lambda i: i
    return count // 16, lambda i: pl.ds(pl.multiple_of(i * 16, 16), 16)


class RingScatter:
    def __init__(self, net, src, pos, to, scratch):
        self.net, self.src, self.pos, self.to = net, src, pos, to
        self.stage, self.halves, self.fulls = scratch

    def block(self, step, half=None):
        return self.src(lax.rem(self.pos + step, RING), half)

    def start(self):
        net, to = self.net, self.to
        self.far = [net.start(self.block(2, 0), self.halves.at[0], to(1)),
                    net.start(self.block(2, 1), self.halves.at[1], to(3))]
        self.full = [net.start(self.block(1, 1), self.fulls.at[0, 1], to(1)),
                     net.start(self.block(3, 0), self.fulls.at[1, 0], to(3))]
        return self

    def relay(self):
        for side in range(2):
            self.far[side].wait_recv()
            term = self.block(1 + 2 * side, side)
            steps, at = chunks(self.stage.shape[1])

            @pl.loop(0, steps)
            def _(i):
                i = at(i)
                self.stage[side, i] = (term[i].astype(f32) + self.halves[side, i].astype(f32)).astype(bf16)

            self.full.append(self.net.start(self.stage.at[side], self.fulls.at[side, side], self.to(1 + 2 * side)))

    def finish(self, store):
        for copy in self.full:
            copy.wait_recv()
        own = self.block(0)
        steps, piece = chunks(self.stage.shape[1])
        _, whole = chunks(own.shape[0])
        for half in range(2):
            @pl.loop(0, steps)
            def _(i):
                at, i = whole(half * steps + i), piece(i)
                store(at, own[at].astype(f32) + self.fulls[0, half, i].astype(f32) + self.fulls[1, half, i].astype(f32))

    def keep(self, target):
        def store(at, total):
            target[at] = total.astype(bf16)

        self.finish(store)


def three(v):
    high = v.astype(bf16)
    rest = v - high.astype(f32)
    middle = rest.astype(bf16)
    low = (rest - middle.astype(f32)).astype(bf16)
    return high, middle, low


def expert_peers(me):
    return [{"expert": lax.rem(me + step, DEVS)} for step in range(1, DEVS)]


def dp_peers(dp):
    return [{"dp": lax.rem(dp + step, GROUPS)} for step in range(1, GROUPS)]


def head_mask(v, head):
    keep = (lanes(v.shape) < HEAD_DIM) == (head == 0)
    return jnp.where(keep, v, jnp.zeros_like(v))


def allowed_rows(begin_ref, start, keys):
    rows = start + lax.broadcasted_iota(jnp.int32, (QB, keys), 0)
    cols = lanes((QB, keys))
    return (cols >= begin_ref[start : start + QB, :1]) & (cols <= rows)


def positions(lengths_ref, rows):
    at = lax.broadcasted_iota(jnp.int32, (rows, 128), 0)
    begin, end = jnp.zeros_like(at), 0
    for i in range(lengths_ref.shape[1]):
        begin = jnp.where(at >= end, end, begin)
        end = end + lengths_ref[0, i]
    return begin, at - begin


def forward(x_ref, gain_one_ref, wq_ref, wkv_ref, wout_ref, lengths_ref, freq_ref, gain_two_ref,
            router_ref, routes_ref, dout_ref, eg_ref, eu_ref, ed_ref,
            group_hbm, wqkv_ref, wo_ref, q_ref, k_ref, v_ref, mixed_ref, lse_ref, cos_ref, sin_ref, begin_ref,
            h_ref, own2_ref, gates_ref, dgate_ref, moe_hbm, dn_hbm, g_hbm, sum0_ref, sum2_ref,
            part, group, n2, dout, gate_buf, own_ref, xs, dos, gs, w_all, local, store_sem,
            net_send, net_recv, *scratch):
    place = Place()
    me, y, z = place.me, place.y, place.z
    greet(expert_peers(me) + dp_peers(place.dp))
    net = Net(net_send, net_recv)
    mine = pl.ds(pl.multiple_of(me * TOK, TOK), TOK)
    ff = eg_ref.shape[2]
    wqkv_ref[y, z, :, :128] = wq_ref[...]
    wqkv_ref[y, z, :, 128:] = wkv_ref[...]
    wo_ref[y, z] = wout_ref[...]
    x = x_ref[...].astype(f32)
    group[mine, :] = (x * rms_scale(x) * gain_one_ref[...]).astype(bf16)
    gather = Gather(net, place, group)
    gather.start()

    def rows_of(half):
        return pl.ds(0, 64) if half is None else pl.ds(half * 32, 32)

    qkv = [net.start(wqkv_ref.at[y, z], wqkv_ref.at[y, z], peer) for peer in dp_peers(place.dp)]
    for e in range(eg_ref.shape[0]):
        for i, ref in enumerate((eg_ref, eu_ref, ed_ref)):
            w_all[e, y, z, :, i * ff : (i + 1) * ff] = ref[e]

    def line(half):
        return pl.ds(0, RING) if half is None else pl.ds(2 * half, 2)

    ones, twos = {}, {}

    def first_ring(e):
        if e < 2:
            ones[e] = RingGather(net, lambda i, half: w_all.at[e, i, z, rows_of(half)], y, place.y_to).start()
        else:
            ones[e] = RingGather(net, lambda i, half: w_all.at[e, y, i, rows_of(half)], z, place.z_to).start()

    def second_ring(e):
        ones[e].finish()
        if e < 2:
            twos[e] = RingGather(net, lambda i, half: w_all.at[e, line(half), i], z, place.z_to).start()
        else:
            twos[e] = RingGather(net, lambda i, half: w_all.at[e, i, line(half)], y, place.y_to).start()

    first_ring(0)
    first_ring(2)
    wo = [net.start(wo_ref.at[y, z], wo_ref.at[y, z], peer) for peer in dp_peers(place.dp)]
    first_ring(1)
    first_ring(3)
    begin, spot = positions(lengths_ref, 1024)
    begin_ref[...] = begin
    angle = spot.astype(f32) * freq_ref[...]
    cos_ref[...] = jnp.cos(angle)
    sine = jnp.sin(angle)
    sin_ref[...] = jnp.where((lanes(sine.shape) & 32) == 0, -sine, sine)
    gather.relay()
    ones[0].relay()
    ones[2].relay()
    gather.last()
    second_ring(0)
    second_ring(2)
    gather.finish()
    ones[1].relay()
    ones[3].relay()
    keep_group = pltpu.make_async_copy(group, group_hbm, local.at[0])
    keep_group.start()
    for copy in qkv:
        copy.wait_recv()
    lin = mm(group[...], wqkv_ref[...].reshape(1024, 256))
    dout[mine, :] = dout_ref[...]
    dout_gather = Gather(net, place, dout)
    dout_gather.start()
    cosine, sine = cos_ref[...], sin_ref[...]

    def rot(v):
        return (v * cosine + swap_halves(v) * sine).astype(bf16)

    q_ref[...] = rot(lin[:, :128])
    kv = lin[:, 128:]
    turned = pltpu.roll(kv, HEAD_DIM, 1)
    low = lanes(kv.shape) < HEAD_DIM
    k_ref[...] = rot(jnp.where(low, kv, turned))
    v_ref[...] = jnp.where(low, turned, kv).astype(bf16)
    for copy in wo:
        copy.wait_recv()
    w_out = wo_ref[...].reshape(1024, 128)
    scatter = Scatter(net, place, part, scratch[:4])
    scratch_rings = scratch[4:]
    for chip in range(RING):
        start, keys = chip * QB, (chip + 1) * QB
        allowed = allowed_rows(begin_ref, start, keys)
        q_blk = q_ref[start:keys, :] * 0.125
        outs, lses = [], []
        for head in range(2):
            scores = mm(head_mask(q_blk, head), k_ref[:keys, :], NT)
            scores = jnp.where(allowed, scores, -1e30)
            top = jnp.max(scores, axis=1, keepdims=True)
            expo = jnp.exp(scores - top)
            total = jnp.sum(expo, axis=1, keepdims=True)
            outs.append(mm(expo.astype(bf16), v_ref[:keys, :]) / total)
            lses.append(top + jnp.log(total))
        first = lanes((QB, 128)) < HEAD_DIM
        mixed_ref[start:keys, :] = jnp.where(first, outs[0], outs[1]).astype(bf16)
        lse_ref[start:keys, :] = jnp.where(first, lses[0], lses[1])
        part[start:keys, :] = mm(mixed_ref[start:keys, :], w_out, NT).astype(bf16)
        scatter.start(chip)
        if chip == 1:
            dout_gather.relay()
        if chip == 2:
            dout_gather.last()
    scatter.far()
    twos[0].relay()
    twos[2].relay()
    second_ring(1)
    second_ring(3)
    dout_gather.finish()
    scatter.near()
    h_one = x + scatter.finish()
    h_ref[...] = h_one
    normed2 = (h_one * rms_scale(h_one) * gain_two_ref[...]).astype(bf16)
    n2[mine, :] = normed2
    own2_ref[...] = normed2
    gather = Gather(net, place, n2)
    gather.start()
    logits = sum(mm(piece, normed2, NT) for piece in three(router_ref[...]))
    n_exp = logits.shape[0]
    each = lax.broadcasted_iota(jnp.int32, logits.shape, 0)
    named = each == routes_ref[0:1, :]
    for r in range(1, routes_ref.shape[0]):
        named = named | (each == routes_ref[r : r + 1, :])
    logits = jnp.where(named, logits, -1e30)
    expo = jnp.where(named, jnp.exp(logits - jnp.max(logits, axis=0, keepdims=True)), 0.0)
    gates = expo / jnp.sum(expo, axis=0, keepdims=True)
    gates_ref[...] = gates
    earlier = lax.broadcasted_iota(jnp.int32, (TOK, TOK), 0) < lanes((TOK, TOK))
    rank = mm(named.astype(f32).astype(bf16), earlier.astype(f32).astype(bf16))
    rank = jnp.where(named, rank, -1.0)
    exp_dev = n_exp // DEVS
    for dev in range(DEVS):
        gate_buf[dev, :exp_dev] = gates[dev * exp_dev : (dev + 1) * exp_dev]
        gate_buf[dev, exp_dev:] = rank[dev * exp_dev : (dev + 1) * exp_dev]
    copies = [net.start(gate_buf.at[peer["expert"]], own_ref.at[me], peer) for peer in expert_peers(me)]
    own_ref[me] = gate_buf[me]
    gather.relay()
    gather.last()
    gather.finish()
    for copy in copies:
        copy.wait_recv()

    def chosen(e, b):
        at = own_ref[b, pl.ds(exp_dev + e, 1), :].astype(jnp.int32)
        return lax.broadcasted_iota(jnp.int32, (CAP, TOK), 0) == at

    @pl.loop(0, DEVS)
    def _(b):
        at = pl.ds(pl.multiple_of(b * TOK, TOK), TOK)
        to = pl.ds(pl.multiple_of(b * CAP, 16), CAP)
        hits = [chosen(e, b) for e in range(exp_dev)]
        pick = jnp.concatenate(hits, axis=0).astype(f32).astype(bf16)
        taken = mm(pick, n2[at, :]).astype(bf16)
        cot = mm(pick, dout[at, :]).astype(bf16)
        for e in range(exp_dev):
            gate = jnp.sum(jnp.where(hits[e], own_ref[b, e : e + 1, :], 0.0), axis=1, keepdims=True)
            xs[e, to, :] = taken[e * CAP : (e + 1) * CAP]
            dos[e, to, :] = cot[e * CAP : (e + 1) * CAP]
            gs[e, to, :] = jnp.broadcast_to(gate, (CAP, 128))

    def run(e):
        twos[e].finish()
        ones[e].drain()
        twos[e].drain()

        def weight(first, count):
            return w_all[e, :, :, :, first * ff : (first + count) * ff].reshape(1024, count * ff)

        def keep(first, count, value):
            w_all[e, :, :, :, first * ff : (first + count) * ff] = value.astype(bf16).reshape(RING, RING, 64, count * ff)

        rows = xs[e]
        gate = gs[e][:, :1]
        both_in = mm(rows, weight(0, 2))
        gate_in, up_in = both_in[:, :ff], both_in[:, ff:]
        sig = jax.nn.sigmoid(gate_in)
        act = gate_in * sig
        hid = (act * up_in).astype(bf16)
        out = mm(hid, weight(2, 1), NT).astype(bf16).astype(f32)
        cot = dos[e].astype(f32)
        d_gate = jnp.sum(out * cot, axis=1, keepdims=True)
        for b in range(DEVS):
            dgate_ref[b, e : e + 1, :] = jnp.sum(
                jnp.where(chosen(e, b), d_gate[b * CAP : (b + 1) * CAP], 0.0), axis=0, keepdims=True)
        d_exp = (cot * gate).astype(bf16)
        dos[e] = (out * gate).astype(bf16)
        dh = mm(d_exp, weight(2, 1))
        keep(2, 1, mm(d_exp, hid, TN))
        dg = (dh * up_in * sig * (1.0 + gate_in * (1.0 - sig))).astype(bf16)
        du = (dh * act).astype(bf16)
        both = jnp.concatenate([dg, du], axis=1)
        xs[e] = mm(both, weight(0, 2), NT).astype(bf16)
        keep(0, 2, mm(rows, both, TN))

    def store(e, slot):
        copy = pltpu.make_async_copy(w_all.at[e], g_hbm.at[slot], store_sem.at[slot])
        copy.start()
        return copy

    rings = [scratch_rings[:3], scratch_rings[3:]]
    twos[1].relay()
    twos[3].relay()
    run(0)
    sums = [RingScatter(net, lambda i, half: w_all.at[0, i, line(half)], y, place.y_to, rings[0]).start()]
    run(2)
    sums.append(RingScatter(net, lambda i, half: w_all.at[2, line(half), i], z, place.z_to, rings[1]).start())
    run(1)
    stores = [store(1, 0)]
    for ring in sums:
        ring.relay()
    run(3)
    stores.append(store(3, 1))
    dout_gather.drain()
    gather.drain()

    @pl.loop(0, DEVS)
    def _(b):
        at = pl.ds(pl.multiple_of(b * TOK, TOK), TOK)
        to = pl.ds(pl.multiple_of(b * CAP, 16), CAP)
        pick = jnp.concatenate([chosen(e, b) for e in range(exp_dev)], axis=0).astype(f32).astype(bf16)
        for source, target in ((xs, n2), (dos, dout)):
            slots = jnp.concatenate([source[e, to, :] for e in range(exp_dev)], axis=0)
            target[at, :] = mm(pick, slots, TN).astype(bf16)

    keep_dn = pltpu.make_async_copy(n2, dn_hbm, local.at[1])
    keep_dn.start()
    keep_moe = pltpu.make_async_copy(dout, moe_hbm, local.at[2])
    keep_moe.start()
    for ring, target in zip(sums, (sum0_ref, sum2_ref)):
        ring.keep(target)
    net.drain()
    for store in stores:
        store.wait()
    keep_group.wait()
    keep_dn.wait()
    keep_moe.wait()


def backward(dn_ref, dgate_ref, dout_ref, h_ref, n2_ref, gates_ref, gain_two_ref, router_ref,
             x_hbm, wqkv_ref, wo_ref, q_ref, k_ref, v_ref, mixed_ref, lse_ref, cos_ref, sin_ref, begin_ref,
             moe_ref, in_ref, gain_one_ref, sum0_ref, sum2_ref, g_ref,
             out_ref, in_grad_ref, gain_one_out, gain_two_out, router_out, gq_ref, gkv_ref, go_ref, gg_ref, gu_ref, gd_ref,
             group, x_ref, dm_ref, dk_ref, dv_ref, both_ref, part, sum1_ref, sum3_ref, gate_got, small, small_got, total, total_z, total_got,
             grads_o, grads_o_got, grads_x, grads_x_got, local, net_send, net_recv, *scratch):
    place = Place()
    me, dp, y, z = place.me, place.dp, place.y, place.z
    greet(expert_peers(me) + dp_peers(dp))
    net = Net(net_send, net_recv)
    load_x = pltpu.make_async_copy(x_hbm, x_ref, local)
    load_x.start()
    dn, moe, scatter = (Scatter(net, place, ref, scratch[4 * i : 4 * i + 4])
                        for i, ref in enumerate((dn_ref, moe_ref, part)))
    rest = scratch[12:]
    ring_one = {1: rest[:3], 3: rest[3:6]}
    ring_two = [rest[6 + 3 * e : 9 + 3 * e] for e in range(4)]
    ring_sums = [sum0_ref, sum1_ref, sum2_ref, sum3_ref]
    for chip in range(RING):
        dn.start(chip)

    def line(half):
        return pl.ds(0, RING) if half is None else pl.ds(2 * half, 2)

    def first_ring(e):
        if e < 2:
            return RingScatter(net, lambda i, half: g_ref.at[0, i, line(half)], y, place.y_to, ring_one[e]).start()
        return RingScatter(net, lambda i, half: g_ref.at[1, line(half), i], z, place.z_to, ring_one[e]).start()

    def second_ring(e):
        own = ring_sums[e]
        if e in ones:
            ones[e].keep(own)

        def piece(i, half):
            return own.at[i] if half is None else own.at[i, pl.ds(half * 32, 32)]

        if e < 2:
            return RingScatter(net, piece, z, place.z_to, ring_two[e]).start()
        return RingScatter(net, piece, y, place.y_to, ring_two[e]).start()

    ones, twos = {}, {}
    for e in (0, 2):
        twos[e] = second_ring(e)
    copies = [net.start(dgate_ref.at[peer["expert"]], gate_got.at[me], peer) for peer in expert_peers(me)]
    gate_got[me] = dgate_ref[me]
    for e in (1, 3):
        ones[e] = first_ring(e)
    dn.far()
    for copy in copies:
        copy.wait_recv()
    dn.near()
    d_gates = jnp.concatenate([gate_got[dev] for dev in range(DEVS)], axis=0)
    gates = gates_ref[...]
    d_logits = gates * (d_gates - jnp.sum(gates * d_gates, axis=0, keepdims=True))
    high, middle, low = three(d_logits)
    r_high, r_middle, _ = three(router_ref[...])
    d_router = mm(jnp.concatenate([high, middle, high], axis=0),
                  jnp.concatenate([r_high, r_high, r_middle], axis=0), TN)
    h_one = h_ref[...]
    scale = rms_scale(h_one)
    d_normed2 = dn.finish() + d_router
    gain = gain_two_ref[...]
    d_h = (dout_ref[...].astype(f32) + scale * (gain * d_normed2)
           - h_one * scale**3 * jnp.mean(h_one * gain * d_normed2, axis=-1, keepdims=True))
    in_grad_ref[...] = d_h
    group[pl.ds(pl.multiple_of(me * TOK, TOK), TOK), :] = d_h.astype(bf16)
    gather = Gather(net, place, group)
    gather.start()
    for chip in range(RING):
        moe.start(chip)
    router_part = sum(mm(piece, n2_ref[...]) for piece in (high, middle, low))
    small[...] = jnp.zeros_like(small)
    for dev in range(DEVS):
        small[dev, :4, :] = router_part[dev * 4 : dev * 4 + 4, :]
    small[0, 4:5, :] = jnp.sum(d_normed2 * h_one * scale, axis=0, keepdims=True)
    twos[0].relay()
    gather.relay()
    twos[2].relay()
    gather.last()
    gather.finish()
    w_out = wo_ref[...].reshape(1024, 128)
    dm_ref[...] = mm(group[...], w_out).astype(bf16)
    grads_o[...] = mm(group[...], mixed_ref[...], TN).astype(bf16).reshape(GROUPS, 64, 128)
    attn = [net.start(grads_o.at[peer["dp"]], grads_o_got.at[dp], peer) for peer in dp_peers(dp)]
    grads_o_got[dp] = grads_o[dp]
    dk_ref[...] = jnp.zeros_like(dk_ref)
    dv_ref[...] = jnp.zeros_like(dv_ref)
    load_x.wait()
    first = lanes((QB, 128)) < HEAD_DIM
    gain_sum = jnp.zeros((1, 1024), f32)
    for chip in reversed(range(RING)):
        start, keys = chip * QB, (chip + 1) * QB
        allowed = allowed_rows(begin_ref, start, keys)
        q_blk = q_ref[start:keys, :] * 0.125
        dm_blk = dm_ref[start:keys, :]
        product = dm_blk.astype(f32) * mixed_ref[start:keys, :].astype(f32)
        dqs = []
        for head in range(2):
            q_head = head_mask(q_blk, head)
            dm_head = head_mask(dm_blk, head)
            scores = mm(q_head, k_ref[:keys, :], NT)
            lse = lse_ref[start:keys, head * HEAD_DIM : head * HEAD_DIM + 1]
            probs = jnp.where(allowed, jnp.exp(scores - lse), 0.0)
            d_probs = mm(dm_head, v_ref[:keys, :], NT)
            delta = jnp.sum(head_mask(product, head), axis=1, keepdims=True)
            d_scores = (probs * (d_probs - delta)).astype(bf16)
            dqs.append(mm(d_scores, k_ref[:keys, :]))
            dk_ref[:keys, :] += mm(d_scores, q_head, TN)
            dv_ref[:keys, :] += mm(probs.astype(bf16), dm_head, TN)
        cosine, sine = cos_ref[start:keys, :], sin_ref[start:keys, :]

        def back(v):
            return v * cosine - swap_halves(v) * sine

        dq = back(jnp.where(first, dqs[0], dqs[1]) * 0.125)
        dk = dk_ref[start:keys, :]
        dk = back(dk + pltpu.roll(dk, HEAD_DIM, 1))
        dv = dv_ref[start:keys, :]
        dv = dv + pltpu.roll(dv, HEAD_DIM, 1)
        both_ref[start:keys, :128] = dq.astype(bf16)
        both_ref[start:keys, 128:] = jnp.where(first, dk, dv).astype(bf16)
        d_rows = mm(both_ref[start:keys, :], wqkv_ref[...].reshape(1024, 256), NT)
        part[start:keys, :] = d_rows.astype(bf16)
        scatter.start(chip)
        gain_sum = gain_sum + jnp.sum(d_rows * x_ref[start:keys, :].astype(f32), axis=0, keepdims=True)
        if chip == 3:
            moe.far()
            ones[1].relay()
            ones[3].relay()
        if chip == 2:
            moe.near()
        if chip == 1:
            out_ref[...] = (h_one + moe.finish()).astype(bf16)
            twos[1] = second_ring(1)
            twos[3] = second_ring(3)
    small[1, 4:5, :] = gain_sum / gain_one_ref[...]
    smalls = [net.start(small.at[peer["expert"]], small_got.at[me], peer) for peer in expert_peers(me)]
    small_got[me] = small[me]
    scatter.far()
    grads_x[...] = mm(x_ref[...], both_ref[...], TN).astype(bf16).reshape(GROUPS, 64, 256)
    attn += [net.start(grads_x.at[peer["dp"]], grads_x_got.at[dp], peer) for peer in dp_peers(dp)]
    grads_x_got[dp] = grads_x[dp]
    scatter.near()
    for copy in smalls:
        copy.wait_recv()
    total[y] = sum(small_got[dev] for dev in range(DEVS))
    sums = [net.start(total.at[y], total.at[y], place.y_to(step)) for step in range(1, RING)]
    twos[1].relay()
    twos[3].relay()
    for copy in sums:
        copy.wait_recv()
    total_z[z] = sum(total[i] for i in range(RING))
    sums = [net.start(total_z.at[z], total_z.at[z], place.z_to(step)) for step in range(1, RING)]
    x = in_ref[...].astype(f32)
    scale, gain = rms_scale(x), gain_one_ref[...]
    d_normed1 = scatter.finish()
    in_grad_ref[...] += (scale * (gain * d_normed1)
                         - x * scale**3 * jnp.mean(x * gain * d_normed1, axis=-1, keepdims=True))
    for copy in sums:
        copy.wait_recv()
    total_got[me] = sum(total_z[i] for i in range(RING))
    spread = [net.start(total_got.at[me], total_got.at[me], peer) for peer in expert_peers(me)]

    def store(e):
        def put(at, value):
            gg_ref[e, at, :] = value[:, :512]
            gu_ref[e, at, :] = value[:, 512:1024]
            gd_ref[e, at, :] = value[:, 1024:]

        return put

    for e in (0, 2, 1, 3):
        twos[e].finish(store(e))
    for copy in attn:
        copy.wait_recv()
    go_ref[...] = sum(grads_o_got[i].astype(f32) for i in range(GROUPS))
    attn_sum = sum(grads_x_got[i].astype(f32) for i in range(GROUPS))
    gq_ref[...] = attn_sum[:, :128]
    gkv_ref[...] = attn_sum[:, 128:]
    for copy in spread:
        copy.wait_recv()
    gain_two_out[...] = total_got[0, 4:5, :]
    gain_one_out[...] = total_got[1, 4:5, :]
    for dev in range(DEVS):
        router_out[dev * 4 : dev * 4 + 4, :] = total_got[dev, :4, :]
    net.drain()


def hand_over(*refs):
    count = len(refs) // 2
    for i in range(count):
        refs[count + i][...] = refs[i][...]


def any_space():
    return pl.BlockSpec(memory_space=pl.ANY)


def params(collective_id=None):
    if collective_id is None:
        return pltpu.CompilerParams(vmem_limit_bytes=VMEM_LIMIT)
    return pltpu.CompilerParams(vmem_limit_bytes=VMEM_LIMIT, collective_id=collective_id, has_side_effects=True)


def cost(flops, nbytes, trans=0):
    return pl.CostEstimate(flops=flops, bytes_accessed=nbytes, transcendentals=trans)


def sds(*shape, dtype=f32):
    return jax.ShapeDtypeStruct(shape, dtype)


def net_sems(count):
    return [pltpu.SemaphoreType.DMA((count,)), pltpu.SemaphoreType.DMA((count,))]


def body(block_input, attn_gain, query_weight, kv_weight, out_weight, moe_gain, router_weight,
         expert_gate, expert_up, expert_down, routes, seq_lengths, out_grad):
    tok, width = block_input.shape
    exp_dev, _, ff = expert_gate.shape
    n_exp = exp_dev * DEVS
    rows = tok * DEVS

    half = HEAD_DIM // 2
    inv_freq = jnp.exp(-jnp.log(rope_base) * 2.0 * jnp.arange(half, dtype=f32) / HEAD_DIM)
    freq = jnp.tile(inv_freq, 4)[None, :]
    gain_one, gain_two = attn_gain[None, :], moe_gain[None, :]
    router = router_weight.T

    wide = sds(rows, 128, dtype=bf16)
    table = sds(rows, 128)
    whole_shape = sds(rows, width, dtype=bf16)
    kept = sds(exp_dev // 2, RING, RING, 64, 3 * ff, dtype=bf16)
    ring_sum = sds(RING, 64, 3 * ff, dtype=bf16)
    buffer = pltpu.VMEM((rows, width), bf16)
    slots = DEVS * CAP
    ring_shape, last_shape = (RING, 64, 3 * ff), (64, 3 * ff)
    (group_in, w_qkv, w_o, queries, keys, values, mixed, lse, cosine, sine, begin, h_one, normed2, gates, d_gate,
     moe_part, dn_part, g_kept, sum0, sum2) = pl.pallas_call(
        forward,
        out_shape=(whole_shape, sds(RING, RING, 64, 256, dtype=bf16), sds(RING, RING, 64, 128, dtype=bf16),
                   wide, wide, wide, wide, table, table, table, sds(rows, 128, dtype=jnp.int32),
                   sds(tok, width), sds(tok, width, dtype=bf16),
                   sds(n_exp, tok), sds(DEVS, exp_dev, tok), whole_shape, whole_shape, kept, ring_sum, ring_sum),
        in_specs=[vmem()] * 5 + [pl.BlockSpec(memory_space=pltpu.SMEM)] + [vmem()] * 8,
        out_specs=(any_space(),) + (vmem(),) * 14 + (any_space(),) * 3 + (vmem(),) * 2,
        scratch_shapes=[buffer, buffer, buffer, buffer, pltpu.VMEM((DEVS, 2 * exp_dev, tok), f32),
                        pltpu.VMEM((DEVS, 2 * exp_dev, tok), f32),
                        pltpu.VMEM((exp_dev, slots, width), bf16), pltpu.VMEM((exp_dev, slots, width), bf16),
                        pltpu.VMEM((exp_dev, slots, 128), f32),
                        pltpu.VMEM((exp_dev, RING, RING, 64, 3 * ff), bf16),
                        pltpu.SemaphoreType.DMA((3,)), pltpu.SemaphoreType.DMA((2,)),
                        *net_sems(160), *scatter_scratch(), *ring_scratch(ring_shape), *ring_scratch(ring_shape)],
        compiler_params=params(1),
        cost_estimate=cost(20 * 10**9, 10**8, 2 * 10**6),
        name="forward",
    )(block_input, gain_one, query_weight, kv_weight, out_weight, seq_lengths, freq, gain_two, router,
      routes.T, out_grad, expert_gate, expert_up, expert_down)

    attn_grad = sds(64, 128)
    expert_grad = sds(exp_dev, 64, ff)
    rings = ring_scratch(ring_shape) + ring_scratch(ring_shape)
    for _ in range(exp_dev):
        rings += ring_scratch(last_shape)
    shapes = (sds(tok, width, dtype=bf16), sds(tok, width), sds(1, width), sds(1, width), sds(n_exp, width),
              attn_grad, attn_grad, attn_grad, expert_grad, expert_grad, expert_grad)
    outs = pl.pallas_call(
        backward,
        out_shape=shapes,
        in_specs=[vmem()] * 8 + [any_space()] + [vmem()] * 16,
        out_specs=(vmem(),) * 11,
        scratch_shapes=[buffer, buffer, pltpu.VMEM((rows, 128), bf16), pltpu.VMEM((rows, 128), f32),
                        pltpu.VMEM((rows, 128), f32), pltpu.VMEM((rows, 256), bf16), buffer,
                        pltpu.VMEM(ring_shape, bf16), pltpu.VMEM(ring_shape, bf16),
                        pltpu.VMEM((DEVS, exp_dev, tok), f32),
                        pltpu.VMEM((DEVS, 8, width), f32), pltpu.VMEM((DEVS, 8, width), f32),
                        pltpu.VMEM((RING, 8, width), f32), pltpu.VMEM((RING, 8, width), f32),
                        pltpu.VMEM((DEVS, 8, width), f32),
                        pltpu.VMEM((GROUPS, 64, 128), bf16), pltpu.VMEM((GROUPS, 64, 128), bf16),
                        pltpu.VMEM((GROUPS, 64, 256), bf16), pltpu.VMEM((GROUPS, 64, 256), bf16),
                        pltpu.SemaphoreType.DMA, *net_sems(160),
                        *scatter_scratch(), *scatter_scratch(), *scatter_scratch(), *rings],
        compiler_params=params(2),
        cost_estimate=cost(5 * 10**9, 10**8, 2 * 10**6),
        name="backward",
    )(dn_part, d_gate, out_grad, h_one, normed2, gates, gain_two, router, group_in, w_qkv, w_o, queries, keys,
      values, mixed, lse, cosine, sine, begin, moe_part, block_input, gain_one, sum0, sum2, g_kept)
    (block_out, input_grad, gain_one_grad, gain_two_grad, router_grad, g_query, g_kv, g_out, g_gate, g_up,
     g_down) = pl.pallas_call(
        hand_over,
        out_shape=shapes,
        in_specs=[vmem()] * len(shapes),
        out_specs=(vmem(),) * len(shapes),
        cost_estimate=cost(0, 10**7, 0),
        name="hand_over",
    )(*outs)
    return (block_out, input_grad, gain_one_grad[0], g_query, g_kv, g_out, gain_two_grad[0], router_grad.T,
            g_gate, g_up, g_down)


def solution(mesh):
    token = P(("dp", "expert"), None)
    attn = P("dp", "expert")
    expert = P("expert", "dp", None)
    return jax.shard_map(
        body,
        mesh=mesh,
        in_specs=(token, P(), attn, attn, attn, P(), P(), expert, expert, expert, token, P("dp", None), token),
        out_specs=(token, token, P(), attn, attn, attn, P(), P(), expert, expert, expert),
        check_vma=False,
    )
```

```python
import functools

import jax
import jax.numpy as jnp
from jax import lax
from jax.experimental import pallas as pl
from jax.experimental.pallas import tpu as pltpu
from jax.sharding import PartitionSpec as P

HEAD_DIM = 64
HIGH = lax.Precision.HIGHEST
eps_norm = 1e-06
rope_base = 10000.0
f32 = jnp.float32
bf16 = jnp.bfloat16
NT = (((1,), (1,)), ((), ()))
TN = (((0,), (0,)), ((), ()))
QB = 256
CAP = 48
VMEM_LIMIT = 60 * 1024 * 1024


def rms_scale(v):
    return lax.rsqrt(jnp.mean(v * v, axis=-1, keepdims=True) + eps_norm)


def mm(a, b, dims=(((1,), (0,)), ((), ()))):
    return lax.dot_general(a, b, dims, preferred_element_type=f32)


def vmem():
    return pl.BlockSpec(memory_space=pltpu.VMEM)


def lanes(shape):
    return lax.broadcasted_iota(jnp.int32, shape, len(shape) - 1)


def swap_halves(v):
    low = (lanes(v.shape) & 32) == 0
    return jnp.where(low, pltpu.roll(v, 96, 1), pltpu.roll(v, 32, 1))


MESH = pl.DeviceIdType.MESH
TOK = 128
HALF = TOK // 2
RING = 4
DEVS = 8
GROUPS = 16
LOADED = 15


class Place:
    def __init__(self):
        self.me, self.dp = lax.axis_index("expert"), lax.axis_index("dp")
        self.chip, self.core = lax.div(self.me, 2), lax.rem(self.me, 2)
        self.y, self.z = lax.div(self.dp, RING), lax.rem(self.dp, RING)

    def at(self, step, other=False):
        return lax.rem(self.chip + step, RING) * 2 + (1 - self.core if other else self.core)

    def x_to(self, step, other=False):
        return {"expert": self.at(step, other)}

    def y_to(self, step):
        return {"dp": lax.rem(self.y + step, RING) * RING + self.z}

    def z_to(self, step):
        return {"dp": self.y * RING + lax.rem(self.z + step, RING)}


def greet(peers):
    barrier = pltpu.get_barrier_semaphore()
    for peer in peers:
        pl.semaphore_signal(barrier, inc=1, device_id=peer, device_id_type=MESH)
    pl.semaphore_wait(barrier, len(peers))


class Net:
    def __init__(self, send, recv):
        self.send, self.recv, self.used, self.sent = send, recv, 0, []

    def take(self, count):
        self.used += count
        return self.used - count

    def copy(self, src, dst, to, slot):
        return pltpu.make_async_remote_copy(
            src_ref=src, dst_ref=dst, send_sem=self.send.at[slot], recv_sem=self.recv.at[slot],
            device_id=to, device_id_type=MESH)

    def start(self, src, dst, to, slot=None):
        copy = self.copy(src, dst, to, self.take(1) if slot is None else slot)
        copy.start()
        self.sent.append(copy)
        return copy

    def drain(self):
        for copy in self.sent:
            copy.wait_send()

    def drain_some(self, copies):
        for copy in copies:
            copy.wait_send()
            self.sent = [other for other in self.sent if other is not copy]


def shard(buf, index, half=None):
    first = index * TOK + (HALF if half == 1 else 0)
    count = TOK if half is None else HALF
    return buf.at[pl.ds(pl.multiple_of(first, HALF), count), :]


class Gather:
    def __init__(self, net, place, buf):
        self.net, self.place, self.buf, self.sent = net, place, buf, []

    def send(self, index, to, half=None):
        piece = shard(self.buf, index, half)
        self.sent.append(self.net.start(piece, piece, to))
        return self.sent[-1]

    def drain(self):
        self.net.drain_some(self.sent)

    def start(self):
        p = self.place
        self.from_left = self.send(p.me, p.x_to(1))
        self.from_right = self.send(p.me, p.x_to(3))
        self.from_sib = self.send(p.me, p.x_to(0, True))

    def relay(self):
        p, sib = self.place, self.place.x_to(0, True)
        self.from_left.wait_recv()
        self.top = self.send(p.at(3), p.x_to(1), 0)
        self.left_sib = self.send(p.at(3), sib)
        self.from_right.wait_recv()
        self.bottom = self.send(p.at(1), p.x_to(3), 1)
        self.right_sib = self.send(p.at(1), sib)

    def last(self):
        p, sib = self.place, self.place.x_to(0, True)
        self.top.wait_recv()
        self.top_sib = self.send(p.at(2), sib, 0)
        self.bottom.wait_recv()
        self.bottom_sib = self.send(p.at(2), sib, 1)

    def finish(self):
        for copy in (self.from_sib, self.left_sib, self.right_sib, self.top_sib, self.bottom_sib):
            copy.wait_recv()


def scatter_scratch():
    return [pltpu.VMEM((RING, TOK, 1024), bf16), pltpu.VMEM((RING, TOK, 1024), bf16),
            pltpu.VMEM((2, HALF, 1024), bf16), pltpu.VMEM((2, TOK, 1024), bf16)]


class Scatter:
    def __init__(self, net, place, part, scratch):
        self.net, self.place, self.part = net, place, part
        self.from_sib, self.mine, self.halves, self.fulls = scratch
        self.slots = net.take(RING)

    def start(self, chip):
        src = shard(self.part, 2 * chip + 1 - self.place.core)
        self.net.start(src, self.from_sib.at[chip], self.place.x_to(0, True), self.slots + chip)

    def chip_sum(self, step):
        p = self.place
        index = p.at(step)
        chip = lax.div(index, 2)
        src = shard(self.part, index)
        self.net.copy(src, self.from_sib.at[chip], p.x_to(0, True), self.slots + chip).wait_recv()
        self.mine[step] = (src[...].astype(f32) + self.from_sib[chip].astype(f32)).astype(bf16)

    def send(self, step, half, dst, to):
        return self.net.start(self.mine.at[step, pl.ds(half * HALF, HALF), :], dst, to)

    def far(self):
        p = self.place
        self.chip_sum(2)
        self.via_right = self.send(2, 0, self.halves.at[0], p.x_to(1))
        self.via_left = self.send(2, 1, self.halves.at[1], p.x_to(3))
        self.chip_sum(1)
        self.right_bottom = self.send(1, 1, self.fulls.at[0, pl.ds(HALF, HALF), :], p.x_to(1))
        self.chip_sum(3)
        self.left_top = self.send(3, 0, self.fulls.at[1, pl.ds(0, HALF), :], p.x_to(3))
        self.chip_sum(0)

    def near(self):
        p = self.place
        self.via_right.wait_recv()
        self.mine[1, :HALF] = (self.mine[1, :HALF].astype(f32) + self.halves[0].astype(f32)).astype(bf16)
        self.right_top = self.send(1, 0, self.fulls.at[0, pl.ds(0, HALF), :], p.x_to(1))
        self.via_left.wait_recv()
        self.mine[3, HALF:] = (self.mine[3, HALF:].astype(f32) + self.halves[1].astype(f32)).astype(bf16)
        self.left_bottom = self.send(3, 1, self.fulls.at[1, pl.ds(HALF, HALF), :], p.x_to(3))

    def finish(self):
        for copy in (self.right_bottom, self.left_top, self.right_top, self.left_bottom):
            copy.wait_recv()
        return self.mine[0].astype(f32) + self.fulls[0].astype(f32) + self.fulls[1].astype(f32)


class RingGather:
    def __init__(self, net, piece, pos, to):
        self.net, self.piece, self.pos, self.to, self.sent = net, piece, pos, to, []

    def send(self, step, half, to):
        piece = self.piece(lax.rem(self.pos + step, RING), half)
        self.sent.append(self.net.start(piece, piece, self.to(to)))
        return self.sent[-1]

    def drain(self):
        self.net.drain_some(self.sent)

    def start(self):
        self.from_left, self.from_right = self.send(0, None, 1), self.send(0, None, 3)
        return self

    def relay(self):
        self.from_left.wait_recv()
        self.top = self.send(3, 0, 1)
        self.from_right.wait_recv()
        self.bottom = self.send(1, 1, 3)

    def finish(self):
        self.top.wait_recv()
        self.bottom.wait_recv()


def ring_scratch(shape):
    half = (shape[0] // 2, *shape[1:])
    return [pltpu.VMEM((2, *half), bf16), pltpu.VMEM((2, *half), bf16), pltpu.VMEM((2, 2, *half), bf16)]


def chunks(count):
    if count <= RING:
        return count, lambda i: i
    return count // 16, lambda i: pl.ds(pl.multiple_of(i * 16, 16), 16)


class RingScatter:
    def __init__(self, net, src, pos, to, scratch):
        self.net, self.src, self.pos, self.to = net, src, pos, to
        self.stage, self.halves, self.fulls = scratch

    def block(self, step, half=None):
        return self.src(lax.rem(self.pos + step, RING), half)

    def start(self):
        net, to = self.net, self.to
        self.far = [net.start(self.block(2, 0), self.halves.at[0], to(1)),
                    net.start(self.block(2, 1), self.halves.at[1], to(3))]
        self.full = [net.start(self.block(1, 1), self.fulls.at[0, 1], to(1)),
                     net.start(self.block(3, 0), self.fulls.at[1, 0], to(3))]
        return self

    def relay(self):
        for side in range(2):
            self.far[side].wait_recv()
            term = self.block(1 + 2 * side, side)
            steps, at = chunks(self.stage.shape[1])

            @pl.loop(0, steps)
            def _(i):
                i = at(i)
                self.stage[side, i] = (term[i].astype(f32) + self.halves[side, i].astype(f32)).astype(bf16)

            self.full.append(self.net.start(self.stage.at[side], self.fulls.at[side, side], self.to(1 + 2 * side)))

    def finish(self, store):
        for copy in self.full:
            copy.wait_recv()
        own = self.block(0)
        steps, piece = chunks(self.stage.shape[1])
        _, whole = chunks(own.shape[0])
        for half in range(2):
            @pl.loop(0, steps)
            def _(i):
                at, i = whole(half * steps + i), piece(i)
                store(at, own[at].astype(f32) + self.fulls[0, half, i].astype(f32) + self.fulls[1, half, i].astype(f32))

    def keep(self, target):
        def store(at, total):
            target[at] = total.astype(bf16)

        self.finish(store)


def line(half):
    return pl.ds(0, RING) if half is None else pl.ds(2 * half, 2)


def first_rings(net, place, grads, scratch):
    return [RingScatter(net, lambda i, half: grads.at[i, line(half), pl.ds(0, 32)], place.y, place.y_to, scratch[:3]).start(),
            RingScatter(net, lambda i, half: grads.at[line(half), i, pl.ds(32, 32)], place.z, place.z_to, scratch[3:]).start()]


def last_rings(net, place, sums, scratch):
    def piece(part):
        return lambda i, half: sums.at[part, i] if half is None else sums.at[part, i, pl.ds(half * 16, 16)]

    return [RingScatter(net, piece(0), place.z, place.z_to, scratch[:3]).start(),
            RingScatter(net, piece(1), place.y, place.y_to, scratch[3:]).start()]


def three(v):
    high = v.astype(bf16)
    rest = v - high.astype(f32)
    middle = rest.astype(bf16)
    low = (rest - middle.astype(f32)).astype(bf16)
    return high, middle, low


def expert_peers(me):
    return [{"expert": lax.rem(me + step, DEVS)} for step in range(1, DEVS)]


def dp_peers(dp):
    return [{"dp": lax.rem(dp + step, GROUPS)} for step in range(1, GROUPS)]


def head_mask(v, head):
    keep = (lanes(v.shape) < HEAD_DIM) == (head == 0)
    return jnp.where(keep, v, jnp.zeros_like(v))


def allowed_rows(begin_ref, start, keys):
    rows = start + lax.broadcasted_iota(jnp.int32, (QB, keys), 0)
    cols = lanes((QB, keys))
    return (cols >= begin_ref[start : start + QB, :1]) & (cols <= rows)


def positions(lengths_ref, rows):
    at = lax.broadcasted_iota(jnp.int32, (rows, 128), 0)
    begin, end = jnp.zeros_like(at), 0
    for i in range(lengths_ref.shape[1]):
        begin = jnp.where(at >= end, end, begin)
        end = end + lengths_ref[0, i]
    return begin, at - begin


def forward(x_ref, gain_one_ref, wq_ref, wkv_ref, wout_ref, lengths_ref, freq_ref, gain_two_ref,
            router_ref, routes_ref, dout_ref, eg_ref, eu_ref, ed_ref,
            group_hbm, h_ref, own2_ref, gates_ref, dgot_ref, dn_ref, sum0_ref, sum2_ref, moe_hbm, g_hbm, *refs):
    held_hbm, held = refs[:10], refs[10:20]
    wqkv_ref, wo_ref, q_ref, k_ref, v_ref, mixed_ref, lse_ref, cos_ref, sin_ref, begin_ref = held
    (part, group, n2, dout, gate_buf, gate_own, rank_buf, rank_own, dgate, xs, dos, gs, w_all, local, store_sem,
     keep_sem, net_send, net_recv, *scratch) = refs[20:]
    place = Place()
    me, y, z = place.me, place.y, place.z
    greet(expert_peers(me) + dp_peers(place.dp))
    net = Net(net_send, net_recv)
    mine = pl.ds(pl.multiple_of(me * TOK, TOK), TOK)
    ff = eg_ref.shape[2]
    wqkv_ref[y, z, :, :128] = wq_ref[...]
    wqkv_ref[y, z, :, 128:] = wkv_ref[...]
    wo_ref[y, z] = wout_ref[...]
    x = x_ref[...].astype(f32)
    group[mine, :] = (x * rms_scale(x) * gain_one_ref[...]).astype(bf16)
    gather = Gather(net, place, group)
    gather.start()

    def rows_of(half):
        return pl.ds(0, 64) if half is None else pl.ds(half * 32, 32)

    qkv = [net.start(wqkv_ref.at[y, z], wqkv_ref.at[y, z], peer) for peer in dp_peers(place.dp)]
    for e in range(eg_ref.shape[0]):
        for i, ref in enumerate((eg_ref, eu_ref, ed_ref)):
            w_all[e, y, z, :, i * ff : (i + 1) * ff] = ref[e]

    ones, twos = {}, {}

    def first_ring(e):
        if e < 2:
            ones[e] = RingGather(net, lambda i, half: w_all.at[e, i, z, rows_of(half)], y, place.y_to).start()
        else:
            ones[e] = RingGather(net, lambda i, half: w_all.at[e, y, i, rows_of(half)], z, place.z_to).start()

    def second_ring(e):
        ones[e].finish()
        if e < 2:
            twos[e] = RingGather(net, lambda i, half: w_all.at[e, line(half), i], z, place.z_to).start()
        else:
            twos[e] = RingGather(net, lambda i, half: w_all.at[e, i, line(half)], y, place.y_to).start()

    first_ring(0)
    first_ring(2)
    exp_dev = dgate.shape[1]
    each = lax.broadcasted_iota(jnp.int32, (DEVS * exp_dev, TOK), 0)
    named = each == routes_ref[0:1, :]
    for r in range(1, routes_ref.shape[0]):
        named = named | (each == routes_ref[r : r + 1, :])
    earlier = lax.broadcasted_iota(jnp.int32, (TOK, TOK), 0) < lanes((TOK, TOK))
    rank = mm(named.astype(f32).astype(bf16), earlier.astype(f32).astype(bf16))
    rank = jnp.where(named, rank, -1.0)
    for dev in range(DEVS):
        rank_buf[dev] = rank[dev * exp_dev : (dev + 1) * exp_dev]
    ranks = [net.start(rank_buf.at[peer["expert"]], rank_own.at[me], peer) for peer in expert_peers(me)]
    rank_own[me] = rank_buf[me]
    begin, spot = positions(lengths_ref, 1024)
    begin_ref[...] = begin
    entry = lax.broadcasted_iota(jnp.int32, (64, 128), 0)
    angle = jnp.where(entry < 32, entry * 32, entry - 32).astype(f32) * freq_ref[...]
    cosine, sine = jnp.cos(angle), jnp.sin(angle)
    coarse = (entry < 32).astype(f32)
    table = jnp.concatenate([cosine * coarse, sine * coarse, cosine * (1.0 - coarse), sine * (1.0 - coarse)], axis=1)
    lane = lanes((1024, 128))
    spot = jnp.where(lane < 32, spot // 32, spot % 32 + 32)
    wanted = (spot == lane).astype(f32).astype(bf16)[:, :64]
    far_cos, far_sin, near_cos, near_sin = jnp.split(sum(mm(wanted, piece) for piece in three(table)), 4, axis=1)
    cos_ref[...] = far_cos * near_cos - far_sin * near_sin
    sine = far_sin * near_cos + far_cos * near_sin
    sin_ref[...] = jnp.where((lane & 32) == 0, -sine, sine)
    gather.relay()
    gather.last()
    wo = [net.start(wo_ref.at[y, z], wo_ref.at[y, z], peer) for peer in dp_peers(place.dp)]
    ones[0].relay()
    ones[2].relay()
    first_ring(1)
    first_ring(3)
    gather.finish()
    keep_group = pltpu.make_async_copy(group, group_hbm, local.at[0])
    keep_group.start()
    for copy in qkv:
        copy.wait_recv()
    lin = mm(group[...], wqkv_ref[...].reshape(1024, 256))
    dout[mine, :] = dout_ref[...]
    dout_gather = Gather(net, place, dout)
    dout_gather.start()
    cosine, sine = cos_ref[...], sin_ref[...]

    def rot(v):
        return (v * cosine + swap_halves(v) * sine).astype(bf16)

    q_ref[...] = rot(lin[:, :128])
    kv = lin[:, 128:]
    turned = pltpu.roll(kv, HEAD_DIM, 1)
    low = lanes(kv.shape) < HEAD_DIM
    k_ref[...] = rot(jnp.where(low, kv, turned))
    v_ref[...] = jnp.where(low, turned, kv).astype(bf16)
    second_ring(0)
    second_ring(2)
    for copy in wo:
        copy.wait_recv()
    w_out = wo_ref[...].reshape(1024, 128)
    scatter = Scatter(net, place, part, scratch[:4])
    scratch_dn, scratch_rings = scratch[4:8], scratch[8:]
    for chip in range(RING):
        start, keys = chip * QB, (chip + 1) * QB
        allowed = allowed_rows(begin_ref, start, keys)
        q_blk = q_ref[start:keys, :] * 0.125
        outs, lses = [], []
        for head in range(2):
            scores = mm(head_mask(q_blk, head), k_ref[:keys, :], NT)
            scores = jnp.where(allowed, scores, -1e30)
            top = jnp.max(scores, axis=1, keepdims=True)
            expo = jnp.exp(scores - top)
            total = jnp.sum(expo, axis=1, keepdims=True)
            outs.append(mm(expo.astype(bf16), v_ref[:keys, :]) / total)
            lses.append(top + jnp.log(total))
        first = lanes((QB, 128)) < HEAD_DIM
        mixed_ref[start:keys, :] = jnp.where(first, outs[0], outs[1]).astype(bf16)
        lse_ref[start:keys, :] = jnp.where(first, lses[0], lses[1])
        part[start:keys, :] = mm(mixed_ref[start:keys, :], w_out, NT).astype(bf16)
        scatter.start(chip)
        if chip == 1:
            dout_gather.relay()
            ones[1].relay()
            ones[3].relay()
        if chip == 2:
            dout_gather.last()
    scatter.far()
    second_ring(1)
    second_ring(3)
    twos[0].relay()
    twos[2].relay()
    keeps = [pltpu.make_async_copy(source, target, keep_sem.at[i]) for i, (source, target) in enumerate(zip(held, held_hbm))]
    for keep_held in keeps:
        keep_held.start()
    dout_gather.finish()
    scatter.near()
    h_one = x + scatter.finish()
    h_ref[...] = h_one
    normed2 = (h_one * rms_scale(h_one) * gain_two_ref[...]).astype(bf16)
    n2[mine, :] = normed2
    own2_ref[...] = normed2
    gather = Gather(net, place, n2)
    gather.start()
    logits = sum(mm(piece, normed2, NT) for piece in three(router_ref[...]))
    logits = jnp.where(named, logits, -1e30)
    expo = jnp.where(named, jnp.exp(logits - jnp.max(logits, axis=0, keepdims=True)), 0.0)
    gates = expo / jnp.sum(expo, axis=0, keepdims=True)
    gates_ref[...] = gates
    for dev in range(DEVS):
        gate_buf[dev] = gates[dev * exp_dev : (dev + 1) * exp_dev]
    copies = [net.start(gate_buf.at[peer["expert"]], gate_own.at[me], peer) for peer in expert_peers(me)]
    gate_own[me] = gate_buf[me]

    def chosen(e, b):
        at = rank_own[b, pl.ds(e, 1), :].astype(jnp.int32)
        return lax.broadcasted_iota(jnp.int32, (CAP, TOK), 0) == at

    def picks(b):
        return jnp.concatenate([chosen(e, b) for e in range(exp_dev)], axis=0).astype(f32).astype(bf16)

    def take(source, target):
        @pl.loop(0, DEVS)
        def _(b):
            at = pl.ds(pl.multiple_of(b * TOK, TOK), TOK)
            to = pl.ds(pl.multiple_of(b * CAP, 16), CAP)
            taken = mm(picks(b), source[at, :]).astype(bf16)
            for e in range(exp_dev):
                target[e, to, :] = taken[e * CAP : (e + 1) * CAP]

    def give(source, target):
        @pl.loop(0, DEVS)
        def _(b):
            at = pl.ds(pl.multiple_of(b * TOK, TOK), TOK)
            to = pl.ds(pl.multiple_of(b * CAP, 16), CAP)
            slots = jnp.concatenate([source[e, to, :] for e in range(exp_dev)], axis=0)
            target[at, :] = mm(picks(b), slots, TN).astype(bf16)

    for copy in ranks:
        copy.wait_recv()
    take(dout, dos)
    gather.relay()
    gather.last()
    gather.finish()
    for copy in copies:
        copy.wait_recv()

    @pl.loop(0, DEVS)
    def _(b):
        to = pl.ds(pl.multiple_of(b * CAP, 16), CAP)
        for e in range(exp_dev):
            gate = jnp.sum(jnp.where(chosen(e, b), gate_own[b, e : e + 1, :], 0.0), axis=1, keepdims=True)
            gs[e, to, :] = jnp.broadcast_to(gate, (CAP, 128))

    take(n2, xs)

    def run(e):
        twos[e].finish()
        ones[e].drain()
        twos[e].drain()

        def weight(first, count):
            return w_all[e, :, :, :, first * ff : (first + count) * ff].reshape(1024, count * ff)

        def keep(first, count, value):
            w_all[e, :, :, :, first * ff : (first + count) * ff] = value.astype(bf16).reshape(RING, RING, 64, count * ff)

        rows = xs[e]
        gate = gs[e][:, :1]
        both_in = mm(rows, weight(0, 2))
        gate_in, up_in = both_in[:, :ff], both_in[:, ff:]
        sig = jax.nn.sigmoid(gate_in)
        act = gate_in * sig
        hid = (act * up_in).astype(bf16)
        out = mm(hid, weight(2, 1), NT).astype(bf16).astype(f32)
        cot = dos[e].astype(f32)
        d_gate = jnp.sum(out * cot, axis=1, keepdims=True)
        for b in range(DEVS):
            dgate[b, e : e + 1, :] = jnp.sum(
                jnp.where(chosen(e, b), d_gate[b * CAP : (b + 1) * CAP], 0.0), axis=0, keepdims=True)
        d_exp = (cot * gate).astype(bf16)
        dos[e] = (out * gate).astype(bf16)
        dh = mm(d_exp, weight(2, 1))
        keep(2, 1, mm(d_exp, hid, TN))
        dg = (dh * up_in * sig * (1.0 + gate_in * (1.0 - sig))).astype(bf16)
        du = (dh * act).astype(bf16)
        both = jnp.concatenate([dg, du], axis=1)
        xs[e] = mm(both, weight(0, 2), NT).astype(bf16)
        keep(0, 2, mm(rows, both, TN))

    def store(e, slot):
        copy = pltpu.make_async_copy(w_all.at[e], g_hbm.at[slot], store_sem.at[slot])
        copy.start()
        return copy

    twos[1].relay()
    twos[3].relay()
    run(0)
    sums0 = first_rings(net, place, w_all.at[0], scratch_rings[:6])
    run(2)
    for ring in sums0:
        ring.relay()
    sums2 = first_rings(net, place, w_all.at[2], scratch_rings[6:])
    run(1)
    stores = [store(1, 0)]
    for ring in sums2:
        ring.relay()
    run(3)
    stores.append(store(3, 1))
    d_gates = [net.start(dgate.at[peer["expert"]], dgot_ref.at[me], peer) for peer in expert_peers(me)]
    dgot_ref[me] = dgate[me]
    dout_gather.drain()
    gather.drain()
    give(xs, n2)
    dn = Scatter(net, place, n2, scratch_dn)
    for chip in range(RING):
        dn.start(chip)
    give(dos, dout)
    keep_moe = pltpu.make_async_copy(dout, moe_hbm, local.at[1])
    keep_moe.start()
    dn.far()
    for part_of, ring in enumerate(sums0):
        ring.keep(sum0_ref.at[part_of])
    dn.near()
    for part_of, ring in enumerate(sums2):
        ring.keep(sum2_ref.at[part_of])
    dn_ref[...] = dn.finish()
    for copy in d_gates:
        copy.wait_recv()
    net.drain()
    for store in stores:
        store.wait()
    keep_group.wait()
    keep_moe.wait()
    for keep_held in keeps:
        keep_held.wait()


def backward(dn_ref, dgot_ref, dout_ref, h_ref, n2_ref, gates_ref, gain_two_ref, router_ref, in_ref, gain_one_ref,
             *refs):
    loaded, outs, rest = refs[:LOADED], refs[LOADED : LOADED + 11], refs[LOADED + 11 :]
    held, rest = rest[:LOADED], rest[LOADED:]
    out_ref, in_grad_ref, gain_one_out, gain_two_out, router_out, gq_ref, gkv_ref, go_ref, gg_ref, gu_ref, gd_ref = outs
    (sum0_ref, sum2_ref, g_ref, moe_ref, wo_ref, mixed_ref, x_ref, wqkv_ref, q_ref, k_ref, v_ref, lse_ref, cos_ref,
     sin_ref, begin_ref) = held
    (group, dm_ref, dk_ref, dv_ref, both_ref, part, sum1_ref, sum3_ref, small, small_got, total, total_z, total_got,
     grads_o, grads_o_got, grads_x, grads_x_got, load_sem, net_send, net_recv, *scratch) = rest
    place = Place()
    me, dp, y, z = place.me, place.dp, place.y, place.z
    greet(expert_peers(me) + dp_peers(dp))
    net = Net(net_send, net_recv)
    loads = [pltpu.make_async_copy(source, target, load_sem.at[i]) for i, (source, target) in enumerate(zip(loaded, held))]
    for load in loads:
        load.start()
    moe, scatter = Scatter(net, place, moe_ref, scratch[:4]), Scatter(net, place, part, scratch[4:8])
    rest = scratch[8:]
    ring_sums = [sum0_ref, sum1_ref, sum2_ref, sum3_ref]

    def last(e):
        return last_rings(net, place, ring_sums[e], rest[12 + 6 * e : 18 + 6 * e])

    def relay(rings):
        for ring in rings:
            ring.relay()

    def keep(e):
        for part_of, ring in enumerate(ones[e]):
            ring.keep(ring_sums[e].at[part_of])

    def store(e, part_of):
        def put(at, value):
            rows = pl.ds(pl.multiple_of(part_of * 32 + at.start, 16), 16)
            gg_ref[e, rows, :] = value[:, :512]
            gu_ref[e, rows, :] = value[:, 512:1024]
            gd_ref[e, rows, :] = value[:, 1024:]

        return put

    def finish(e):
        for part_of, ring in enumerate(twos[e]):
            ring.finish(store(e, part_of))

    ones, twos = {}, {}
    d_gates = jnp.concatenate([dgot_ref[dev] for dev in range(DEVS)], axis=0)
    gates = gates_ref[...]
    d_logits = gates * (d_gates - jnp.sum(gates * d_gates, axis=0, keepdims=True))
    high, middle, low = three(d_logits)
    r_high, r_middle, _ = three(router_ref[...])
    d_router = mm(jnp.concatenate([high, middle, high], axis=0),
                  jnp.concatenate([r_high, r_high, r_middle], axis=0), TN)
    h_one = h_ref[...]
    scale = rms_scale(h_one)
    d_normed2 = dn_ref[...] + d_router
    gain = gain_two_ref[...]
    d_h = (dout_ref[...].astype(f32) + scale * (gain * d_normed2)
           - h_one * scale**3 * jnp.mean(h_one * gain * d_normed2, axis=-1, keepdims=True))
    in_grad_ref[...] = d_h
    group[pl.ds(pl.multiple_of(me * TOK, TOK), TOK), :] = d_h.astype(bf16)
    gather = Gather(net, place, group)
    gather.start()
    for i in range(2):
        loads[i].wait()
    twos[0], twos[2] = last(0), last(2)
    loads[2].wait()
    ones[1] = first_rings(net, place, g_ref.at[0], rest[:6])
    ones[3] = first_rings(net, place, g_ref.at[1], rest[6:12])
    loads[3].wait()
    for chip in range(RING):
        moe.start(chip)
    router_part = sum(mm(piece, n2_ref[...]) for piece in (high, middle, low))
    small[...] = jnp.zeros_like(small)
    for dev in range(DEVS):
        small[dev, :4, :] = router_part[dev * 4 : dev * 4 + 4, :]
    small[0, 4:5, :] = jnp.sum(d_normed2 * h_one * scale, axis=0, keepdims=True)
    gather.relay()
    gather.last()
    relay(twos[0])
    relay(twos[2])
    gather.finish()
    for i in range(4, LOADED):
        loads[i].wait()
    w_out = wo_ref[...].reshape(1024, 128)
    dm_ref[...] = mm(group[...], w_out).astype(bf16)
    grads_o[...] = mm(group[...], mixed_ref[...], TN).astype(bf16).reshape(GROUPS, 64, 128)
    attn = [net.start(grads_o.at[peer["dp"]], grads_o_got.at[dp], peer) for peer in dp_peers(dp)]
    grads_o_got[dp] = grads_o[dp]
    dk_ref[...] = jnp.zeros_like(dk_ref)
    dv_ref[...] = jnp.zeros_like(dv_ref)
    relay(ones[1])
    relay(ones[3])
    first = lanes((QB, 128)) < HEAD_DIM
    gain_sum = jnp.zeros((1, 1024), f32)
    for chip in reversed(range(RING)):
        start, keys = chip * QB, (chip + 1) * QB
        allowed = allowed_rows(begin_ref, start, keys)
        q_blk = q_ref[start:keys, :] * 0.125
        dm_blk = dm_ref[start:keys, :]
        product = dm_blk.astype(f32) * mixed_ref[start:keys, :].astype(f32)
        dqs = []
        for head in range(2):
            q_head = head_mask(q_blk, head)
            dm_head = head_mask(dm_blk, head)
            scores = mm(q_head, k_ref[:keys, :], NT)
            lse = lse_ref[start:keys, head * HEAD_DIM : head * HEAD_DIM + 1]
            probs = jnp.where(allowed, jnp.exp(scores - lse), 0.0)
            d_probs = mm(dm_head, v_ref[:keys, :], NT)
            delta = jnp.sum(head_mask(product, head), axis=1, keepdims=True)
            d_scores = (probs * (d_probs - delta)).astype(bf16)
            dqs.append(mm(d_scores, k_ref[:keys, :]))
            dk_ref[:keys, :] += mm(d_scores, q_head, TN)
            dv_ref[:keys, :] += mm(probs.astype(bf16), dm_head, TN)
        cosine, sine = cos_ref[start:keys, :], sin_ref[start:keys, :]

        def back(v):
            return v * cosine - swap_halves(v) * sine

        dq = back(jnp.where(first, dqs[0], dqs[1]) * 0.125)
        dk = dk_ref[start:keys, :]
        dk = back(dk + pltpu.roll(dk, HEAD_DIM, 1))
        dv = dv_ref[start:keys, :]
        dv = dv + pltpu.roll(dv, HEAD_DIM, 1)
        both_ref[start:keys, :128] = dq.astype(bf16)
        both_ref[start:keys, 128:] = jnp.where(first, dk, dv).astype(bf16)
        d_rows = mm(both_ref[start:keys, :], wqkv_ref[...].reshape(1024, 256), NT)
        part[start:keys, :] = d_rows.astype(bf16)
        scatter.start(chip)
        gain_sum = gain_sum + jnp.sum(d_rows * x_ref[start:keys, :].astype(f32), axis=0, keepdims=True)
        if chip == 3:
            moe.far()
        if chip == 2:
            moe.near()
            keep(1)
            twos[1] = last(1)
        if chip == 1:
            out_ref[...] = (h_one + moe.finish()).astype(bf16)
            keep(3)
            twos[3] = last(3)
    small[1, 4:5, :] = gain_sum / gain_one_ref[...]
    smalls = [net.start(small.at[peer["expert"]], small_got.at[me], peer) for peer in expert_peers(me)]
    small_got[me] = small[me]
    scatter.far()
    grads_x[...] = mm(x_ref[...], both_ref[...], TN).astype(bf16).reshape(GROUPS, 64, 256)
    attn += [net.start(grads_x.at[peer["dp"]], grads_x_got.at[dp], peer) for peer in dp_peers(dp)]
    grads_x_got[dp] = grads_x[dp]
    scatter.near()
    finish(0)
    finish(2)
    for copy in smalls:
        copy.wait_recv()
    total[y] = sum(small_got[dev] for dev in range(DEVS))
    sums = [net.start(total.at[y], total.at[y], place.y_to(step)) for step in range(1, RING)]
    relay(twos[1])
    relay(twos[3])
    for copy in sums:
        copy.wait_recv()
    total_z[z] = sum(total[i] for i in range(RING))
    sums = [net.start(total_z.at[z], total_z.at[z], place.z_to(step)) for step in range(1, RING)]
    x = in_ref[...].astype(f32)
    scale, gain = rms_scale(x), gain_one_ref[...]
    d_normed1 = scatter.finish()
    in_grad_ref[...] += (scale * (gain * d_normed1)
                         - x * scale**3 * jnp.mean(x * gain * d_normed1, axis=-1, keepdims=True))
    for copy in sums:
        copy.wait_recv()
    total_got[me] = sum(total_z[i] for i in range(RING))
    spread = [net.start(total_got.at[me], total_got.at[me], peer) for peer in expert_peers(me)]

    finish(1)
    finish(3)
    for copy in attn:
        copy.wait_recv()
    go_ref[...] = sum(grads_o_got[i].astype(f32) for i in range(GROUPS))
    attn_sum = sum(grads_x_got[i].astype(f32) for i in range(GROUPS))
    gq_ref[...] = attn_sum[:, :128]
    gkv_ref[...] = attn_sum[:, 128:]
    for copy in spread:
        copy.wait_recv()
    gain_two_out[...] = total_got[0, 4:5, :]
    gain_one_out[...] = total_got[1, 4:5, :]
    for dev in range(DEVS):
        router_out[dev * 4 : dev * 4 + 4, :] = total_got[dev, :4, :]
    net.drain()


def hand_over(*refs):
    count = len(refs) // 2
    for i in range(count):
        refs[count + i][...] = refs[i][...]


def any_space():
    return pl.BlockSpec(memory_space=pl.ANY)


def params(collective_id=None):
    if collective_id is None:
        return pltpu.CompilerParams(vmem_limit_bytes=VMEM_LIMIT)
    return pltpu.CompilerParams(vmem_limit_bytes=VMEM_LIMIT, collective_id=collective_id, has_side_effects=True)


def cost(flops, nbytes, trans=0):
    return pl.CostEstimate(flops=flops, bytes_accessed=nbytes, transcendentals=trans)


def sds(*shape, dtype=f32):
    return jax.ShapeDtypeStruct(shape, dtype)


def net_sems(count):
    return [pltpu.SemaphoreType.DMA((count,)), pltpu.SemaphoreType.DMA((count,))]


def body(block_input, attn_gain, query_weight, kv_weight, out_weight, moe_gain, router_weight,
         expert_gate, expert_up, expert_down, routes, seq_lengths, out_grad):
    tok, width = block_input.shape
    exp_dev, _, ff = expert_gate.shape
    n_exp = exp_dev * DEVS
    rows = tok * DEVS

    half = HEAD_DIM // 2
    inv_freq = jnp.exp(-jnp.log(rope_base) * 2.0 * jnp.arange(half, dtype=f32) / HEAD_DIM)
    freq = jnp.tile(inv_freq, 4)[None, :]
    gain_one, gain_two = attn_gain[None, :], moe_gain[None, :]
    router = router_weight.T

    wide = sds(rows, 128, dtype=bf16)
    table = sds(rows, 128)
    whole_shape = sds(rows, width, dtype=bf16)
    kept = sds(exp_dev // 2, RING, RING, 64, 3 * ff, dtype=bf16)
    ring_sum = sds(2, RING, 32, 3 * ff, dtype=bf16)
    buffer = pltpu.VMEM((rows, width), bf16)
    slots = DEVS * CAP
    ring_shape, last_shape = (RING, 32, 3 * ff), (32, 3 * ff)
    held = (sds(RING, RING, 64, 256, dtype=bf16), sds(RING, RING, 64, 128, dtype=bf16), wide, wide, wide, wide,
            table, table, table, sds(rows, 128, dtype=jnp.int32))
    (group_in, h_one, normed2, gates, d_gate, d_normed2, sum0, sum2, moe_part, g_kept, w_qkv, w_o, queries, keys,
     values, mixed, lse, cosine, sine, begin) = pl.pallas_call(
        forward,
        out_shape=(whole_shape, sds(tok, width), sds(tok, width, dtype=bf16), sds(n_exp, tok), sds(DEVS, exp_dev, tok),
                   sds(tok, width), ring_sum, ring_sum, whole_shape, kept, *held),
        in_specs=[vmem()] * 5 + [pl.BlockSpec(memory_space=pltpu.SMEM)] + [vmem()] * 8,
        out_specs=(any_space(),) + (vmem(),) * 7 + (any_space(),) * 12,
        scratch_shapes=[*[pltpu.VMEM(array.shape, array.dtype) for array in held],
                        buffer, buffer, buffer, buffer, *[pltpu.VMEM((DEVS, exp_dev, tok), f32)] * 5,
                        pltpu.VMEM((exp_dev, slots, width), bf16), pltpu.VMEM((exp_dev, slots, width), bf16),
                        pltpu.VMEM((exp_dev, slots, 128), f32),
                        pltpu.VMEM((exp_dev, RING, RING, 64, 3 * ff), bf16),
                        pltpu.SemaphoreType.DMA((2,)), pltpu.SemaphoreType.DMA((2,)), pltpu.SemaphoreType.DMA((10,)),
                        *net_sems(180), *scatter_scratch(), *scatter_scratch(), *ring_scratch(ring_shape) * 4],
        compiler_params=params(1),
        cost_estimate=cost(20 * 10**9, 10**8, 2 * 10**6),
        name="forward",
    )(block_input, gain_one, query_weight, kv_weight, out_weight, seq_lengths, freq, gain_two, router,
      routes.T, out_grad, expert_gate, expert_up, expert_down)

    attn_grad = sds(64, 128)
    expert_grad = sds(exp_dev, 64, ff)
    rings = ring_scratch(ring_shape) * 4 + ring_scratch(last_shape) * 8
    loaded = (sum0, sum2, g_kept, moe_part, w_o, mixed, group_in, w_qkv, queries, keys, values, lse, cosine, sine, begin)
    shapes = (sds(tok, width, dtype=bf16), sds(tok, width), sds(1, width), sds(1, width), sds(n_exp, width),
              attn_grad, attn_grad, attn_grad, expert_grad, expert_grad, expert_grad)
    outs = pl.pallas_call(
        backward,
        out_shape=shapes,
        in_specs=[vmem()] * 10 + [any_space()] * LOADED,
        out_specs=(vmem(),) * 11,
        scratch_shapes=[*[pltpu.VMEM(array.shape, array.dtype) for array in loaded],
                        buffer, pltpu.VMEM((rows, 128), bf16), pltpu.VMEM((rows, 128), f32),
                        pltpu.VMEM((rows, 128), f32), pltpu.VMEM((rows, 256), bf16), buffer,
                        pltpu.VMEM((2, *ring_shape), bf16), pltpu.VMEM((2, *ring_shape), bf16),
                        pltpu.VMEM((DEVS, 8, width), f32), pltpu.VMEM((DEVS, 8, width), f32),
                        pltpu.VMEM((RING, 8, width), f32), pltpu.VMEM((RING, 8, width), f32),
                        pltpu.VMEM((DEVS, 8, width), f32),
                        pltpu.VMEM((GROUPS, 64, 128), bf16), pltpu.VMEM((GROUPS, 64, 128), bf16),
                        pltpu.VMEM((GROUPS, 64, 256), bf16), pltpu.VMEM((GROUPS, 64, 256), bf16),
                        pltpu.SemaphoreType.DMA((LOADED,)), *net_sems(180),
                        *scatter_scratch(), *scatter_scratch(), *rings],
        compiler_params=params(2),
        cost_estimate=cost(5 * 10**9, 10**8, 2 * 10**6),
        name="backward",
    )(d_normed2, d_gate, out_grad, h_one, normed2, gates, gain_two, router, block_input, gain_one, *loaded)
    (block_out, input_grad, gain_one_grad, gain_two_grad, router_grad, g_query, g_kv, g_out, g_gate, g_up,
     g_down) = pl.pallas_call(
        hand_over,
        out_shape=shapes,
        in_specs=[vmem()] * len(shapes),
        out_specs=(vmem(),) * len(shapes),
        cost_estimate=cost(0, 10**7, 0),
        name="hand_over",
    )(*outs)
    return (block_out, input_grad, gain_one_grad[0], g_query, g_kv, g_out, gain_two_grad[0], router_grad.T,
            g_gate, g_up, g_down)


def solution(mesh):
    token = P(("dp", "expert"), None)
    attn = P("dp", "expert")
    expert = P("expert", "dp", None)
    return jax.shard_map(
        body,
        mesh=mesh,
        in_specs=(token, P(), attn, attn, attn, P(), P(), expert, expert, expert, token, P("dp", None), token),
        out_specs=(token, token, P(), attn, attn, attn, P(), P(), expert, expert, expert),
        check_vma=False,
    )
```
